512 devices in a mesh: visit: 64 (over y_hi, z, core), strip: 8 (over x, y_lo).
Axes of the slice: x: 4, y: 8 (y_hi: 4, y_lo: 2; y = y_hi * 2 + y_lo), z: 8, core: 2. Of those that a mesh axis runs over, the one named last changes fastest.
Arguments:
- images: float32 [64, 512, 256], P('visit', 'strip')
- variances: float32 [64, 512, 256], P('visit', 'strip'), may hold values from 0.25 to 4
- masks: int32 [64, 512, 256], P('visit', 'strip'), may hold values from 0 to 4095, as said below
- visit_ids: int32 [64], P('visit'), may hold values from 0 to 63, each once
- kernels: float32 [64, 3, 2, 21], replicated, may hold values from 0.01 to 0.09
- amplitudes: float32 [64, 3], replicated, may hold values from 0.5 to 2
- shapes: float32 [64, 3, 5], replicated, may hold values from -0.18 to 0.18
Outputs:
- coadd: float32 [512, 256], P(('strip', 'visit'))
- depth: float32 [512, 256], P(('strip', 'visit'))
The draws below stay inside these ranges and needn't reach their ends.
Inputs may be any that keep to these rules, and one draw needn't show every extreme that they name: `masks`: A visit pixel is used where bits 0, 1 and 2 of its mask are all clear; bits 3 to 11 are other mask planes. Every pixel is used in at least 3 visits.
All inputs are finite; a program needn't handle non-finite values.
Results may differ from the reference program's by a relative error of at most 0.0003.
Values sent between devices are 32-bit elements; how exact they have to be, the bound alone decides.
No kernel may reach another device: no remote copies, remote signals or barrier semaphores. Data moves between devices by JAX's collectives and lax.ppermute only.
A program may use at most 64 MiB of HBM per device.

```python
import math
import jax
import jax.numpy as jnp
from jax import lax

W = 256
TAPS = 21
BASES = 3
SHAPE_TERMS = 5
VISITS = 64
H = 512


def draw_images(key, part):
    key = jax.random.fold_in(key, 11)
    sky_key = jax.random.fold_in(key, 1)
    noise_key = jax.random.fold_in(key, 2)
    sky = 3.0 * jax.random.normal(sky_key, (H, W), jnp.float32)
    noise = 2.0 * jax.random.normal(noise_key, (VISITS, H, W), jnp.float32)
    return (sky[None, :, :] + noise).astype(jnp.float32)


def draw_masks(key, part):
    key = jax.random.fold_in(key, 23)
    upper = jax.random.randint(jax.random.fold_in(key, 1), (VISITS, H, W), 0, 512)
    bad_one = (jax.random.randint(jax.random.fold_in(key, 2), (VISITS, H, W), 0, 16) == 0).astype(jnp.int32)
    bad_two = (jax.random.randint(jax.random.fold_in(key, 3), (VISITS, H, W), 0, 16) == 0).astype(jnp.int32)
    bad_three = (jax.random.randint(jax.random.fold_in(key, 4), (VISITS, H, W), 0, 16) == 0).astype(jnp.int32)
    shift = jax.random.randint(jax.random.fold_in(key, 5), (1, H, W), 0, VISITS)
    slot = jnp.arange(VISITS, dtype=jnp.int32)[:, None, None]
    kept = (jnp.remainder(slot + shift, VISITS) < 3).astype(jnp.int32)
    bad = (bad_one + 2 * bad_two + 4 * bad_three) * (1 - kept)
    return (upper * 8 + bad).astype(jnp.int32)


def levels(stream_key, shape, split, low, largest):
    def one(axis_at, blocks):
        draws = jax.random.uniform(jax.random.fold_in(jax.random.fold_in(stream_key, 6), axis_at), (blocks,), jnp.float32, low / len(split), largest / len(split))
        return jnp.repeat(jnp.exp(draws), shape[axis_at] // blocks).reshape((-1,) + (1,) * (len(shape) - axis_at - 1))

    loudness = one(*split[0])
    for cut in split[1:]:
        loudness = loudness * one(*cut)
    return loudness


def setup_inputs(seed: int = 0) -> dict:
    arg_keys = jax.random.split(jax.random.key(seed), 8)
    images = draw_images(jax.random.fold_in(arg_keys[7], 71), 0)
    variances = jnp.clip(jnp.exp(math.log(4.0) - 2.7725887 * jax.random.uniform(arg_keys[1], (VISITS, H, W), jnp.float32) ** levels(arg_keys[1], (VISITS, H, W), ((0, 64), (1, 8)), -0.2, 0.2)), 0.25, 4.0)
    masks = draw_masks(jax.random.fold_in(arg_keys[7], 71), 0)
    visit_ids = jax.random.permutation(arg_keys[3], VISITS).astype(jnp.int32)
    kernels = jnp.clip(jax.random.uniform(arg_keys[4], (VISITS, BASES, 2, TAPS), jnp.float32, 0.01, 0.09), 0.01, 0.09)
    amplitudes = jnp.clip(jnp.exp(jax.random.uniform(arg_keys[5], (VISITS, BASES), jnp.float32, math.log(0.5), math.log(2.0))), 0.5, 2.0)
    shapes = jnp.clip(jax.random.uniform(arg_keys[6], (VISITS, BASES, SHAPE_TERMS), jnp.float32, -0.18, 0.18), -0.18, 0.18)
    return dict(images=images, variances=variances, masks=masks, visit_ids=visit_ids, kernels=kernels, amplitudes=amplitudes, shapes=shapes)


pair_first = (0, 1, 2, 0, 0, 1)
pair_second = (0, 1, 2, 1, 2, 2)
pair_count = (1.0, 1.0, 1.0, 2.0, 2.0, 2.0)


def separable(field, row_taps, col_taps, rows):
    span = col_taps.shape[-1]
    half = span // 2
    width = field.shape[-1]
    padded = jnp.pad(field, ((0, 0), (half, half)))
    across = col_taps[:, 0, None, None] * padded[None, :, 0:width]
    for offset in range(1, span):
        across = across + col_taps[:, offset, None, None] * padded[None, :, offset:offset + width]
    down = row_taps[:, 0, None, None] * across[:, 0:rows, :]
    for offset in range(1, span):
        down = down + row_taps[:, offset, None, None] * across[:, offset:offset + rows, :]
    return down


def spatial(amplitude, shape, ys, xs):
    terms = 1.0 + shape[:, 0, None, None] * xs + shape[:, 1, None, None] * ys
    terms = terms + shape[:, 2, None, None] * (xs * xs) + shape[:, 3, None, None] * (xs * ys)
    terms = terms + shape[:, 4, None, None] * (ys * ys)
    return amplitude[:, None, None] * terms


def visit_terms(image_rows, variance_rows, mask, row_taps, col_taps, amplitude, shape, ys, xs, rows):
    basis = separable(image_rows, row_taps, col_taps, rows)
    pair_rows = jnp.stack([row_taps[a] * row_taps[b] for a, b in zip(pair_first, pair_second)])
    pair_cols = jnp.stack([col_taps[a] * col_taps[b] for a, b in zip(pair_first, pair_second)])
    paired = separable(variance_rows, pair_rows, pair_cols, rows)
    factor = spatial(amplitude, shape, ys, xs)
    matched = jnp.sum(factor * basis, axis=0)
    cross = jnp.stack([pair_count[p] * factor[pair_first[p]] * factor[pair_second[p]] for p in range(6)])
    matched_var = jnp.sum(cross * paired, axis=0)
    valid = jnp.bitwise_and(mask, 7) == 0
    weight = valid.astype(jnp.float32) / matched_var
    return matched, weight, valid


def reference(images, variances, masks, visit_ids, kernels, amplitudes, shapes):
    half = TAPS // 2
    ys = ((2 * jnp.arange(H, dtype=jnp.int32) + 1).astype(jnp.float32) / H - 1.0)[:, None]
    xs = ((2 * jnp.arange(W, dtype=jnp.int32) + 1).astype(jnp.float32) / W - 1.0)[None, :]

    def one_visit(carry, index):
        total, weights, low_value, low_weight, high_value, high_weight = carry
        visit = visit_ids[index]
        image_rows = jnp.pad(images[index], ((half, half), (0, 0)))
        variance_rows = jnp.pad(variances[index], ((half, half), (0, 0)))
        taps = kernels[visit]
        matched, weight, valid = visit_terms(image_rows, variance_rows, masks[index], taps[:, 0], taps[:, 1],
                                             amplitudes[visit], shapes[visit], ys, xs, H)
        lower = jnp.logical_and(valid, matched < low_value)
        higher = jnp.logical_and(valid, matched > high_value)
        low_value = jnp.where(lower, matched, low_value)
        low_weight = jnp.where(lower, weight, low_weight)
        high_value = jnp.where(higher, matched, high_value)
        high_weight = jnp.where(higher, weight, high_weight)
        return (total + weight * matched, weights + weight, low_value, low_weight, high_value, high_weight), None

    zeros = jnp.zeros((H, W), jnp.float32)
    start = (zeros, zeros, jnp.full((H, W), jnp.inf, jnp.float32), zeros,
             jnp.full((H, W), -jnp.inf, jnp.float32), zeros)
    result, unused = lax.scan(one_visit, start, jnp.arange(VISITS, dtype=jnp.int32))
    total, weights, low_value, low_weight, high_value, high_weight = result
    coadd = (total - low_weight * low_value - high_weight * high_value) / (weights - low_weight - high_weight)
    depth = jnp.log(weights + 1.0)
    return coadd, depth
```

```python
import jax
import jax.numpy as jnp
from jax import lax
from jax.experimental import pallas as pl
from jax.experimental.pallas import tpu as pltpu
from jax.sharding import PartitionSpec as P

pair_first = (0, 1, 2, 0, 0, 1)
pair_second = (0, 1, 2, 1, 2, 2)
pair_count = (1.0, 1.0, 1.0, 2.0, 2.0, 2.0)

LANES = 128
EDGE = 16
VMEM_LIMIT = 32 * 1024 * 1024


def shifted_halves(left, right, shift):
    if shift == 0:
        return left, right
    lane = lax.broadcasted_iota(jnp.int32, left.shape, 1)
    turned_left = pltpu.roll(left, (-shift) % LANES, 1)
    turned_right = pltpu.roll(right, (-shift) % LANES, 1)
    zero = jnp.zeros_like(left)
    if shift > 0:
        inside = lane < LANES - shift
        return jnp.where(inside, turned_left, turned_right), jnp.where(inside, turned_right, zero)
    inside = lane >= -shift
    return jnp.where(inside, turned_left, zero), jnp.where(inside, turned_right, turned_left)


def match_kernel(
    ids, images, variances, masks, low, high, kernels, amplitudes, shapes, out, fields, across
):
    rows = images.shape[1]
    span = kernels.shape[-1]
    half = span // 2
    strip_row = lax.axis_index("strip") * rows
    height = rows * lax.axis_size("strip")
    width = images.shape[2]

    for index, own in enumerate((images, variances)):
        fields[index, 0:EDGE] = low[index]
        fields[index, EDGE : EDGE + rows] = own[0]
        fields[index, EDGE + rows :] = high[index]

    def row_tap(j, a):
        return kernels[0, j, 0, a]

    def col_tap(j, a):
        return kernels[0, j, 1, a]

    def taps_of(get, maps, a):
        if maps == 3:
            return [get(j, a) for j in range(3)]
        single = [get(j, a) for j in range(3)]
        return [single[p] * single[q] for p, q in zip(pair_first, pair_second)]

    chunk = 16

    def columns(step, carry):
        start = pl.multiple_of(step * chunk, chunk)
        for field, maps, base in ((0, 3, 0), (1, 6, 3)):
            left = fields[field, pl.ds(start, chunk), 0:LANES]
            right = fields[field, pl.ds(start, chunk), LANES:]
            sums = None
            for a in range(span):
                moved = shifted_halves(left, right, a - half)
                taps = taps_of(col_tap, maps, a)
                terms = [[tap * m for m in moved] for tap in taps]
                if sums is None:
                    sums = terms
                else:
                    sums = [[s + t for s, t in zip(ss, tt)] for ss, tt in zip(sums, terms)]
            for j in range(maps):
                for side in range(2):
                    across[base + j, side, pl.ds(start, chunk), :] = sums[j][side]
        return carry

    lax.fori_loop(0, (rows + 2 * EDGE) // chunk, columns, 0)

    block = 16

    def finish(step, carry):
        start = pl.multiple_of(step * block, block)
        row = lax.broadcasted_iota(jnp.int32, (block, LANES), 0) + (start + strip_row)
        y = (2 * row + 1).astype(jnp.float32) / height - 1.0
        for side in range(2):
            col = lax.broadcasted_iota(jnp.int32, (block, LANES), 1) + side * LANES
            x = (2 * col + 1).astype(jnp.float32) / width - 1.0
            xx, xy, yy = x * x, x * y, y * y
            factor = []
            for j in range(3):
                s = [shapes[0, j, t] for t in range(5)]
                terms = 1.0 + s[0] * x + s[1] * y
                terms = terms + s[2] * xx + s[3] * xy
                terms = terms + s[4] * yy
                factor.append(amplitudes[0, 0, j] * terms)
            results = []
            for maps, base in ((3, 0), (6, 3)):
                sums = None
                for a in range(span):
                    taps = taps_of(row_tap, maps, a)
                    terms = [
                        taps[j] * across[base + j, side, pl.ds(start + EDGE - half + a, block), :]
                        for j in range(maps)
                    ]
                    sums = terms if sums is None else [s + t for s, t in zip(sums, terms)]
                results.append(sums)
            basis, paired = results
            matched = factor[0] * basis[0]
            for j in range(1, 3):
                matched = matched + factor[j] * basis[j]
            spread = None
            for p in range(6):
                cross = factor[pair_first[p]] * factor[pair_second[p]]
                if pair_count[p] != 1.0:
                    cross = (pair_count[p] * factor[pair_first[p]]) * factor[pair_second[p]]
                term = cross * paired[p]
                spread = term if spread is None else spread + term
            mask = masks[0, pl.ds(start, block), side * LANES : (side + 1) * LANES]
            valid = jnp.bitwise_and(mask, 7) == 0
            weight = jnp.where(valid, 1.0 / spread, 0.0)
            out[pl.ds(4 * start + side, block, stride=4), :] = matched
            out[pl.ds(4 * start + 2 + side, block, stride=4), :] = weight
        return carry

    lax.fori_loop(0, rows // block, finish, 0)


def owner_kernel(moved, coadd, depth):
    visits = moved.shape[0] // 4
    for side in range(2):
        matched = moved[pl.ds(side, visits, stride=4), :]
        weight = moved[pl.ds(2 + side, visits, stride=4), :]
        valid = weight > 0.0
        visit = lax.broadcasted_iota(jnp.int32, matched.shape, 0)

        def extreme(values, value):
            first = jnp.min(jnp.where(values == value, visit, visits), axis=0, keepdims=True)
            return jnp.sum(jnp.where(visit == first, weight, 0.0), axis=0, keepdims=True)

        low_values = jnp.where(valid, matched, jnp.inf)
        high_values = jnp.where(valid, matched, -jnp.inf)
        low_value = jnp.min(low_values, axis=0, keepdims=True)
        high_value = jnp.max(high_values, axis=0, keepdims=True)
        low_weight = extreme(low_values, low_value)
        high_weight = extreme(high_values, high_value)
        total = jnp.sum(weight * matched, axis=0, keepdims=True)
        weights = jnp.sum(weight, axis=0, keepdims=True)
        lanes = slice(side * LANES, (side + 1) * LANES)
        coadd[:, lanes] = (total - low_weight * low_value - high_weight * high_value) / (
            weights - low_weight - high_weight
        )
        depth[:, lanes] = jnp.log(weights + 1.0)


def matched_and_weight(
    images, variances, masks, visit_ids, kernels, amplitudes, shapes, low, high
):
    rows, width = images.shape[1:]
    full = rows + 2 * EDGE

    def whole(shape):
        return pl.BlockSpec(shape, lambda i, ids: (0,) * len(shape))

    def chosen(shape):
        return pl.BlockSpec(
            shape,
            lambda i, ids: (ids[0],) + (0,) * (len(shape) - 1),
            memory_space=pltpu.SMEM,
        )

    return pl.pallas_call(
        match_kernel,
        grid_spec=pltpu.PrefetchScalarGridSpec(
            num_scalar_prefetch=1,
            grid=(1,),
            in_specs=[
                whole((1, rows, width)),
                whole((1, rows, width)),
                whole((1, rows, width)),
                whole((2, EDGE, width)),
                whole((2, EDGE, width)),
                chosen((1,) + kernels.shape[1:]),
                chosen((1, 1) + amplitudes.shape[1:]),
                chosen((1,) + shapes.shape[1:]),
            ],
            out_specs=whole((4 * rows, LANES)),
            scratch_shapes=[
                pltpu.VMEM((2, full, width), jnp.float32),
                pltpu.VMEM((9, 2, full, LANES), jnp.float32),
            ],
        ),
        out_shape=jax.ShapeDtypeStruct((4 * rows, LANES), jnp.float32),
        compiler_params=pltpu.CompilerParams(vmem_limit_bytes=VMEM_LIMIT),
    )(visit_ids, images, variances, masks, low, high, kernels, amplitudes[:, None], shapes)


def shards(images, variances, masks, visit_ids, kernels, amplitudes, shapes):
    rows, width = images.shape[1:]
    strips = lax.axis_size("strip")
    visits = lax.axis_size("visit")
    bottom = jnp.concatenate([images[:, rows - EDGE :], variances[:, rows - EDGE :]])
    top = jnp.concatenate([images[:, :EDGE], variances[:, :EDGE]])
    low = lax.ppermute(bottom, "strip", [(i, i + 1) for i in range(strips - 1)])
    high = lax.ppermute(top, "strip", [(i + 1, i) for i in range(strips - 1)])
    sent = matched_and_weight(
        images, variances, masks, visit_ids, kernels, amplitudes, shapes, low, high
    )
    moved = lax.all_to_all(
        sent.reshape(rows, 4, LANES), "visit", split_axis=0, concat_axis=0, tiled=True
    )
    vmem = pl.BlockSpec(memory_space=pltpu.VMEM)
    coadd, depth = pl.pallas_call(
        owner_kernel,
        in_specs=[vmem],
        out_specs=[vmem, vmem],
        out_shape=[jax.ShapeDtypeStruct((1, width), jnp.float32)] * 2,
        compiler_params=pltpu.CompilerParams(vmem_limit_bytes=VMEM_LIMIT),
    )(moved.reshape(visits * 4, LANES))
    return coadd, depth


def solution(mesh):
    in_specs = (
        P("visit", "strip", None),
        P("visit", "strip", None),
        P("visit", "strip", None),
        P("visit"),
        P(),
        P(),
        P(),
    )
    out_specs = (P(("strip", "visit"), None), P(("strip", "visit"), None))
    return jax.shard_map(shards, mesh=mesh, in_specs=in_specs, out_specs=out_specs, check_vma=False)
```

```python
import jax
import jax.numpy as jnp
from jax import lax
from jax.experimental import pallas as pl
from jax.experimental.pallas import tpu as pltpu
from jax.sharding import PartitionSpec as P

pair_first = (0, 1, 2, 0, 0, 1)
pair_second = (0, 1, 2, 1, 2, 2)
pair_count = (1.0, 1.0, 1.0, 2.0, 2.0, 2.0)

LANES = 128
EDGE = 16
VMEM_LIMIT = 32 * 1024 * 1024


def shifted_halves(left, right, shift):
    if shift == 0:
        return left, right
    lane = lax.broadcasted_iota(jnp.int32, left.shape, 1)
    turned_left = pltpu.roll(left, (-shift) % LANES, 1)
    turned_right = pltpu.roll(right, (-shift) % LANES, 1)
    zero = jnp.zeros_like(left)
    if shift > 0:
        inside = lane < LANES - shift
        return jnp.where(inside, turned_left, turned_right), jnp.where(inside, turned_right, zero)
    inside = lane >= -shift
    return jnp.where(inside, turned_left, zero), jnp.where(inside, turned_right, turned_left)


def add_terms(sums, terms):
    return terms if sums is None else [s + t for s, t in zip(sums, terms)]


def columns(images, variances, taps, source, across, target, count):
    span = taps.shape[1]
    for field, maps, base in ((images, 3, 0), (variances, 6, 3)):
        left = field[pl.ds(source, count), 0:LANES]
        right = field[pl.ds(source, count), LANES:]
        sums = None
        for a in range(span):
            moved = shifted_halves(left, right, a - span // 2)
            terms = []
            for j in range(base, base + maps):
                tap = taps[j, a, pl.ds(1, 1), :]
                terms += [tap * m for m in moved]
            sums = add_terms(sums, terms)
        for j in range(maps):
            for side in range(2):
                across[base + j, side, pl.ds(target, count), :] = sums[2 * j + side]


def matched_rows(across, taps, coefs, first, count, offsets, row, height, width, store):
    span = taps.shape[1]
    results = []
    for maps, base in ((3, 0), (6, 3)):
        sums = None
        for a, offset in offsets:
            terms = []
            for j in range(base, base + maps):
                tap = taps[j, a, pl.ds(0, 1), :]
                terms += [tap * across[j, side, pl.ds(first + offset, count), :] for side in range(2)]
            sums = add_terms(sums, terms)
        results += sums
    y = (2 * row + 1).astype(jnp.float32) / height - 1.0
    for side in range(2):
        basis, paired = results[side:6:2], results[6 + side :: 2]
        col = lax.broadcasted_iota(jnp.int32, (count, LANES), 1) + side * LANES
        x = (2 * col + 1).astype(jnp.float32) / width - 1.0
        xx, xy, yy = x * x, x * y, y * y
        factor = []
        for j in range(3):
            s = [coefs[pl.ds(3 * t + j, 1), :] for t in range(6)]
            terms = 1.0 + s[0] * x + s[1] * y
            terms = terms + s[2] * xx + s[3] * xy
            terms = terms + s[4] * yy
            factor.append(s[5] * terms)
        matched = factor[0] * basis[0]
        for j in range(1, 3):
            matched = matched + factor[j] * basis[j]
        spread = None
        for p in range(6):
            cross = factor[pair_first[p]]
            if pair_count[p] != 1.0:
                cross = pair_count[p] * cross
            term = cross * factor[pair_second[p]] * paired[p]
            spread = term if spread is None else spread + term
        store(side, matched, spread)


def of_visit(visit, table):
    here = lax.broadcasted_iota(jnp.int32, table.shape, table.ndim - 1) == visit
    value = jnp.sum(jnp.where(here, table, 0.0), axis=-1, keepdims=True)
    return jnp.broadcast_to(value, table.shape[:-1] + (LANES,))


def edge_kernel(
    ids, kernels, amplitudes, shapes, images, variances,
    below, above, edges, taps, coefs,
    padded, image_ends, variance_ends, tap_table, amplitude_table, shape_table, sems,
):
    rows, width = images.shape[1:]
    span = kernels.shape[1]
    half = span // 2
    copies = [
        (kernels, tap_table),
        (amplitudes, amplitude_table),
        (shapes, shape_table),
        (images.at[0, pl.ds(0, EDGE)], image_ends.at[pl.ds(0, EDGE)]),
        (images.at[0, pl.ds(rows - EDGE, EDGE)], image_ends.at[pl.ds(EDGE, EDGE)]),
        (variances.at[0, pl.ds(0, EDGE)], variance_ends.at[pl.ds(0, EDGE)]),
        (variances.at[0, pl.ds(rows - EDGE, EDGE)], variance_ends.at[pl.ds(EDGE, EDGE)]),
    ]
    copies = [pltpu.make_async_copy(a, b, sems.at[i]) for i, (a, b) in enumerate(copies)]
    for copy in copies:
        copy.start()
    strip_row = lax.axis_index("strip") * rows
    height = rows * lax.axis_size("strip")
    zero = jnp.zeros((9, 2, EDGE, LANES), jnp.float32)
    padded[:, :, 0:EDGE] = zero
    padded[:, :, 2 * EDGE : 3 * EDGE] = zero
    for copy in copies:
        copy.wait()

    visit = ids[0]
    taps[0:3] = of_visit(visit, tap_table[...])
    for p, (i, j) in enumerate(zip(pair_first, pair_second)):
        taps[3 + p] = taps[i] * taps[j]
    for t in range(5):
        coefs[3 * t : 3 * t + 3] = of_visit(visit, shape_table[t])
    coefs[15:18] = of_visit(visit, amplitude_table[...])

    for which, out in ((0, below), (1, above)):
        columns(image_ends, variance_ends, taps, which * EDGE, padded, EDGE, EDGE)
        edges[which] = padded[:, :, EDGE : 2 * EDGE]
        if which == 0:
            offsets = [(a, a - half) for a in range(half + 1, span)]
            first, start = 0, -EDGE
        else:
            offsets = [(a, a - half + EDGE) for a in range(0, half)]
            first, start = EDGE, rows
        row = lax.broadcasted_iota(jnp.int32, (EDGE, LANES), 0) + (strip_row + start)

        def store(side, matched, spread):
            out[side] = matched
            out[2 + side] = spread

        matched_rows(padded, taps, coefs, first, EDGE, offsets, row, height, width, store)


def strip_kernel(images, variances, edges, taps, coefs, out, across):
    rows, width = images.shape[1:]
    span = taps.shape[1]
    half = span // 2
    strip_row = lax.axis_index("strip") * rows
    height = rows * lax.axis_size("strip")
    zero = jnp.zeros((9, 2, EDGE, LANES), jnp.float32)
    across[:, :, 0:EDGE] = zero
    across[:, :, EDGE : 2 * EDGE] = edges[0]
    across[:, :, rows : rows + EDGE] = edges[1]
    across[:, :, rows + EDGE :] = zero

    chunk = 16

    def inner(step, carry):
        start = pl.multiple_of(step * chunk, chunk)
        columns(
            images.at[0], variances.at[0], taps, start + EDGE, across, start + 2 * EDGE, chunk
        )
        return carry

    lax.fori_loop(0, (rows - 2 * EDGE) // chunk, inner, 0)

    block = 16

    def finish(step, carry):
        start = pl.multiple_of(step * block, block)
        row = lax.broadcasted_iota(jnp.int32, (block, LANES), 0) + (start + strip_row)
        offsets = [(a, EDGE - half + a) for a in range(span)]

        def store(side, matched, spread):
            out[side, pl.ds(start, block), :] = matched
            out[2 + side, pl.ds(start, block), :] = spread

        matched_rows(across, taps, coefs, start, block, offsets, row, height, width, store)
        return carry

    lax.fori_loop(0, rows // block, finish, 0)


def weight_kernel(own, masks, low, high, out):
    rows = own.shape[1]
    for side in range(2):
        mask = masks[0, :, side * LANES : (side + 1) * LANES]
        for start, extra in ((0, low), (EDGE, None), (rows - EDGE, high)):
            count = EDGE if extra is not None else rows - 2 * EDGE
            matched = own[side, start : start + count, :]
            spread = own[2 + side, start : start + count, :]
            if extra is not None:
                matched = matched + extra[side]
                spread = spread + extra[2 + side]
            valid = jnp.bitwise_and(mask[start : start + count], 7) == 0
            out[pl.ds(4 * start + side, count, stride=4), :] = matched
            out[pl.ds(4 * start + 2 + side, count, stride=4), :] = jnp.where(valid, 1.0 / spread, 0.0)


def owner_kernel(moved, coadd, depth):
    visits = moved.shape[0] // 4
    for side in range(2):
        matched = moved[pl.ds(side, visits, stride=4), :]
        weight = moved[pl.ds(2 + side, visits, stride=4), :]
        valid = weight > 0.0
        visit = lax.broadcasted_iota(jnp.int32, matched.shape, 0)

        def extreme(values, value):
            first = jnp.min(jnp.where(values == value, visit, visits), axis=0, keepdims=True)
            return jnp.sum(jnp.where(visit == first, weight, 0.0), axis=0, keepdims=True)

        low_values = jnp.where(valid, matched, jnp.inf)
        high_values = jnp.where(valid, matched, -jnp.inf)
        low_value = jnp.min(low_values, axis=0, keepdims=True)
        high_value = jnp.max(high_values, axis=0, keepdims=True)
        low_weight = extreme(low_values, low_value)
        high_weight = extreme(high_values, high_value)
        total = jnp.sum(weight * matched, axis=0, keepdims=True)
        weights = jnp.sum(weight, axis=0, keepdims=True)
        lanes = slice(side * LANES, (side + 1) * LANES)
        coadd[:, lanes] = (total - low_weight * low_value - high_weight * high_value) / (
            weights - low_weight - high_weight
        )
        depth[:, lanes] = jnp.log(weights + 1.0)


VMEM = pl.BlockSpec(memory_space=pltpu.VMEM)
HBM = pl.BlockSpec(memory_space=pltpu.HBM)
SMEM = pl.BlockSpec(memory_space=pltpu.SMEM)
PARAMS = pltpu.CompilerParams(vmem_limit_bytes=VMEM_LIMIT)


def f32(*shape):
    return jax.ShapeDtypeStruct(shape, jnp.float32)


def cost(flops):
    return pl.CostEstimate(flops=flops, bytes_accessed=1 << 20, transcendentals=0)


def edge_parts(ids, kernels, amplitudes, shapes, images, variances):
    width = images.shape[2]
    return pl.pallas_call(
        edge_kernel,
        in_specs=[SMEM] + [HBM] * 5,
        out_specs=[VMEM] * 5,
        out_shape=[
            f32(4, EDGE, LANES),
            f32(4, EDGE, LANES),
            f32(2, 9, 2, EDGE, LANES),
            f32(9, *kernels.shape[1:3], LANES),
            f32(18, LANES),
        ],
        scratch_shapes=[
            pltpu.VMEM((9, 2, 3 * EDGE, LANES), jnp.float32),
            pltpu.VMEM((2 * EDGE, width), jnp.float32),
            pltpu.VMEM((2 * EDGE, width), jnp.float32),
            pltpu.VMEM(kernels.shape, jnp.float32),
            pltpu.VMEM(amplitudes.shape, jnp.float32),
            pltpu.VMEM(shapes.shape, jnp.float32),
            pltpu.SemaphoreType.DMA((7,)),
        ],
        compiler_params=PARAMS,
    )(
        ids,
        *(
            pltpu.with_memory_space_constraint(x, pltpu.HBM)
            for x in (kernels, amplitudes, shapes, images, variances)
        ),
    )


def strip_parts(images, variances, edges, taps, coefs):
    rows = images.shape[1]
    return pl.pallas_call(
        strip_kernel,
        in_specs=[VMEM] * 5,
        out_specs=VMEM,
        out_shape=f32(4, rows, LANES),
        scratch_shapes=[pltpu.VMEM((9, 2, rows + 2 * EDGE, LANES), jnp.float32)],
        compiler_params=PARAMS,
        cost_estimate=cost(20_000_000),
    )(images, variances, edges, taps, coefs)


def weighted(own, masks, low, high):
    rows = own.shape[1]
    return pl.pallas_call(
        weight_kernel,
        in_specs=[VMEM] * 4,
        out_specs=VMEM,
        out_shape=f32(4 * rows, LANES),
        compiler_params=PARAMS,
    )(own, masks, low, high)


def owned(moved, width):
    return pl.pallas_call(
        owner_kernel,
        in_specs=[VMEM],
        out_specs=[VMEM, VMEM],
        out_shape=[f32(1, width)] * 2,
        compiler_params=PARAMS,
    )(moved)


def before_exchange(images, variances, masks, visit_ids, kernels, amplitudes, shapes):
    strips = lax.axis_size("strip")
    below, above, edges, taps, coefs = edge_parts(
        visit_ids,
        jnp.transpose(kernels, (1, 3, 2, 0)),
        jnp.transpose(amplitudes, (1, 0)),
        jnp.transpose(shapes, (2, 1, 0)),
        images,
        variances,
    )
    low = lax.ppermute(above, "strip", [(i, i + 1) for i in range(strips - 1)])
    high = lax.ppermute(below, "strip", [(i + 1, i) for i in range(strips - 1)])
    own = strip_parts(images, variances, edges, taps, coefs)
    return weighted(own, masks, low, high)


def shards(images, variances, masks, visit_ids, kernels, amplitudes, shapes):
    rows, width = images.shape[1:]
    visits = lax.axis_size("visit")
    sent = before_exchange(images, variances, masks, visit_ids, kernels, amplitudes, shapes)
    moved = lax.all_to_all(
        sent.reshape(rows, 4, LANES), "visit", split_axis=0, concat_axis=0, tiled=True
    )
    coadd, depth = owned(moved.reshape(visits * 4, LANES), width)
    return coadd, depth


def solution(mesh):
    in_specs = (
        P("visit", "strip", None),
        P("visit", "strip", None),
        P("visit", "strip", None),
        P("visit"),
        P(),
        P(),
        P(),
    )
    out_specs = (P(("strip", "visit"), None), P(("strip", "visit"), None))
    return jax.shard_map(shards, mesh=mesh, in_specs=in_specs, out_specs=out_specs, check_vma=False)
```

```python
import functools

import jax
import jax.numpy as jnp
from jax import lax
from jax.experimental import pallas as pl
from jax.experimental.pallas import tpu as pltpu
from jax.sharding import PartitionSpec as P

pair_first = (0, 1, 2, 0, 0, 1)
pair_second = (0, 1, 2, 1, 2, 2)
pair_count = (1.0, 1.0, 1.0, 2.0, 2.0, 2.0)

LANES = 128
EDGE = 16
VMEM_LIMIT = 32 * 1024 * 1024


def shifted_halves(left, right, shift):
    if shift == 0:
        return left, right
    lane = lax.broadcasted_iota(jnp.int32, left.shape, 1)
    turned_left = pltpu.roll(left, (-shift) % LANES, 1)
    turned_right = pltpu.roll(right, (-shift) % LANES, 1)
    zero = jnp.zeros_like(left)
    if shift > 0:
        inside = lane < LANES - shift
        return jnp.where(inside, turned_left, turned_right), jnp.where(inside, turned_right, zero)
    inside = lane >= -shift
    return jnp.where(inside, turned_left, zero), jnp.where(inside, turned_right, turned_left)


def add_terms(sums, terms):
    return terms if sums is None else [s + t for s, t in zip(sums, terms)]


def columns(images, variances, taps, source, across, target, count):
    span = taps.shape[1]
    for field, maps, base in ((images, 3, 0), (variances, 6, 3)):
        left = field[pl.ds(source, count), 0:LANES]
        right = field[pl.ds(source, count), LANES:]
        sums = None
        for a in range(span):
            moved = shifted_halves(left, right, a - span // 2)
            terms = []
            for j in range(base, base + maps):
                tap = taps[j, a, pl.ds(1, 1), :]
                terms += [tap * m for m in moved]
            sums = add_terms(sums, terms)
        for j in range(maps):
            for side in range(2):
                across[base + j, side, pl.ds(target, count), :] = sums[2 * j + side]


def row_sums(across, taps, down, tiles, offsets):
    tile = 8
    uses = {}
    for t in range(tiles):
        for a, offset in offsets:
            uses.setdefault(tile * t + offset, []).append((t, a))

    def one_map(j, carry):
        tap = {a: taps[j, a, pl.ds(0, 1), :] for a, offset in offsets}
        sums = [[None] * tiles for side in range(2)]
        for place in sorted(uses):
            for side in range(2):
                rows = across[j, side, pl.ds(place, tile), :]
                for t, a in uses[place]:
                    term = tap[a] * rows
                    sums[side][t] = term if sums[side][t] is None else sums[side][t] + term
        for side in range(2):
            for t in range(tiles):
                down[j, side, tile * t : tile * (t + 1), :] = sums[side][t]
        return carry

    lax.fori_loop(0, 9, one_map, 0, unroll=3)


def combine(down, start, count, coefs, row, height, width, store):
    y = (2 * row + 1).astype(jnp.float32) / height - 1.0
    for side in range(2):
        sums = [down[j, side, pl.ds(start, count), :] for j in range(9)]
        basis, paired = sums[:3], sums[3:]
        col = lax.broadcasted_iota(jnp.int32, (count, LANES), 1) + side * LANES
        x = (2 * col + 1).astype(jnp.float32) / width - 1.0
        xx, xy, yy = x * x, x * y, y * y
        factor = []
        for j in range(3):
            s = [coefs[pl.ds(3 * t + j, 1), :] for t in range(6)]
            terms = 1.0 + s[0] * x + s[1] * y
            terms = terms + s[2] * xx + s[3] * xy
            terms = terms + s[4] * yy
            factor.append(s[5] * terms)
        matched = factor[0] * basis[0]
        for j in range(1, 3):
            matched = matched + factor[j] * basis[j]
        spread = None
        for p in range(6):
            cross = factor[pair_first[p]]
            if pair_count[p] != 1.0:
                cross = pair_count[p] * cross
            term = cross * factor[pair_second[p]] * paired[p]
            spread = term if spread is None else spread + term
        store(side, matched, spread)


def of_visit(visit, table):
    here = lax.broadcasted_iota(jnp.int32, table.shape, table.ndim - 1) == visit
    value = jnp.sum(jnp.where(here, table, 0.0), axis=-1, keepdims=True)
    return jnp.broadcast_to(value, table.shape[:-1] + (LANES,))


def load_kernel(
    kernels, amplitudes, shapes, images, variances,
    tap_table, amplitude_table, shape_table, bottom, top, sems,
):
    rows = images.shape[1]
    copies = [
        (images.at[0, pl.ds(rows - EDGE, EDGE)], bottom.at[0]),
        (variances.at[0, pl.ds(rows - EDGE, EDGE)], bottom.at[1]),
        (images.at[0, pl.ds(0, EDGE)], top.at[0]),
        (variances.at[0, pl.ds(0, EDGE)], top.at[1]),
        (kernels, tap_table),
        (amplitudes, amplitude_table),
        (shapes, shape_table),
    ]
    copies = [pltpu.make_async_copy(a, b, sems.at[i]) for i, (a, b) in enumerate(copies)]
    for copy in copies:
        copy.start()
    for copy in copies:
        copy.wait()


def strip_kernel(
    ids, tap_table, amplitude_table, shape_table, images, variances, masks,
    out, taps, coefs, across, down,
):
    rows, width = images.shape[1:]
    span = taps.shape[1]
    half = span // 2
    strip_row = lax.axis_index("strip") * rows
    height = rows * lax.axis_size("strip")
    zero = jnp.zeros((9, 2, EDGE, LANES), jnp.float32)
    across[:, :, 0:EDGE] = zero
    across[:, :, rows + EDGE :] = zero

    visit = ids[0]
    taps[0:3] = of_visit(visit, tap_table[...])
    for p, (i, j) in enumerate(zip(pair_first, pair_second)):
        taps[3 + p] = taps[i] * taps[j]
    for t in range(5):
        coefs[3 * t : 3 * t + 3] = of_visit(visit, shape_table[t])
    coefs[15:18] = of_visit(visit, amplitude_table[...])

    chunk = 32

    def inner(step, carry):
        start = pl.multiple_of(step * chunk, chunk)
        columns(images.at[0], variances.at[0], taps, start, across, start + EDGE, chunk)
        return carry

    lax.fori_loop(0, rows // chunk, inner, 0)
    row_sums(across, taps, down, rows // 8, [(a, EDGE - half + a) for a in range(span)])

    block = 32
    for start in range(0, rows, block):
        row = lax.broadcasted_iota(jnp.int32, (block, LANES), 0) + (start + strip_row)

        def store(side, matched, spread):
            mask = masks[0, pl.ds(start, block), side * LANES : (side + 1) * LANES]
            valid = jnp.bitwise_and(mask, 7) == 0
            out[side, pl.ds(start, block), :] = matched
            out[2 + side, pl.ds(start, block), :] = jnp.where(valid, spread, jnp.inf)

        combine(down, start, block, coefs, row, height, width, store)


def halo_part(halo, taps, coefs, padded, down, rows, width, start, offsets, source, store):
    strip_row = lax.axis_index("strip") * rows
    height = rows * lax.axis_size("strip")
    padded[:, :, EDGE - source : 2 * EDGE - source] = jnp.zeros((9, 2, EDGE, LANES), jnp.float32)
    columns(halo.at[0], halo.at[1], taps, 0, padded, source, EDGE)
    row_sums(padded, taps, down, EDGE // 8, offsets)
    row = lax.broadcasted_iota(jnp.int32, (EDGE, LANES), 0) + (strip_row + start)
    combine(down, 0, EDGE, coefs, row, height, width, store)


def low_kernel(rows, low, taps, coefs, out, padded, down):
    half = taps.shape[1] // 2

    def store(side, matched, spread):
        out[side] = matched
        out[2 + side] = spread

    offsets = [(a, EDGE - half + a) for a in range(half)]
    halo_part(low, taps, coefs, padded, down, rows, low.shape[2], 0, offsets, 0, store)


def weight_kernel(own, first, high, taps, coefs, out, padded, down, last):
    rows = own.shape[1]
    span = taps.shape[1]
    half = span // 2

    def store(side, matched, spread):
        last[side] = matched
        last[2 + side] = spread

    offsets = [(a, a - half) for a in range(half + 1, span)]
    halo_part(
        high, taps, coefs, padded, down, rows, high.shape[2], rows - EDGE, offsets, EDGE, store
    )
    for side in range(2):
        for start, extra in ((0, first), (EDGE, None), (rows - EDGE, last)):
            count = EDGE if extra is not None else rows - 2 * EDGE
            matched = own[side, start : start + count, :]
            spread = own[2 + side, start : start + count, :]
            if extra is not None:
                matched = matched + extra[side]
                spread = spread + extra[2 + side]
            out[pl.ds(4 * start + side, count, stride=4), :] = matched
            out[pl.ds(4 * start + 2 + side, count, stride=4), :] = 1.0 / spread


def owner_kernel(moved, coadd, depth):
    visits = moved.shape[0] // 4
    for side in range(2):
        matched = moved[pl.ds(side, visits, stride=4), :]
        weight = moved[pl.ds(2 + side, visits, stride=4), :]
        valid = weight > 0.0
        visit = lax.broadcasted_iota(jnp.int32, matched.shape, 0)

        def extreme(values, value):
            first = jnp.min(jnp.where(values == value, visit, visits), axis=0, keepdims=True)
            return jnp.sum(jnp.where(visit == first, weight, 0.0), axis=0, keepdims=True)

        low_values = jnp.where(valid, matched, jnp.inf)
        high_values = jnp.where(valid, matched, -jnp.inf)
        low_value = jnp.min(low_values, axis=0, keepdims=True)
        high_value = jnp.max(high_values, axis=0, keepdims=True)
        low_weight = extreme(low_values, low_value)
        high_weight = extreme(high_values, high_value)
        total = jnp.sum(weight * matched, axis=0, keepdims=True)
        weights = jnp.sum(weight, axis=0, keepdims=True)
        lanes = slice(side * LANES, (side + 1) * LANES)
        coadd[:, lanes] = (total - low_weight * low_value - high_weight * high_value) / (
            weights - low_weight - high_weight
        )
        depth[:, lanes] = jnp.log(weights + 1.0)


VMEM = pl.BlockSpec(memory_space=pltpu.VMEM)
HBM = pl.BlockSpec(memory_space=pltpu.HBM)
SMEM = pl.BlockSpec(memory_space=pltpu.SMEM)
PARAMS = pltpu.CompilerParams(vmem_limit_bytes=VMEM_LIMIT)


def f32(*shape):
    return jax.ShapeDtypeStruct(shape, jnp.float32)


def cost(flops):
    return pl.CostEstimate(flops=flops, bytes_accessed=1 << 20, transcendentals=0)


def loaded(kernels, amplitudes, shapes, images, variances):
    width = images.shape[2]
    return pl.pallas_call(
        load_kernel,
        in_specs=[HBM] * 5,
        out_specs=[VMEM] * 5,
        out_shape=[
            f32(*kernels.shape),
            f32(*amplitudes.shape),
            f32(*shapes.shape),
            f32(2, EDGE, width),
            f32(2, EDGE, width),
        ],
        scratch_shapes=[pltpu.SemaphoreType.DMA((7,))],
        compiler_params=PARAMS,
    )(
        *(
            pltpu.with_memory_space_constraint(x, pltpu.HBM)
            for x in (kernels, amplitudes, shapes, images, variances)
        )
    )


def strip_parts(ids, kernels, amplitudes, shapes, images, variances, masks):
    rows = images.shape[1]
    return pl.pallas_call(
        strip_kernel,
        in_specs=[SMEM] + [VMEM] * 6,
        out_specs=[VMEM] * 3,
        out_shape=[f32(4, rows, LANES), f32(9, *kernels.shape[1:3], LANES), f32(18, LANES)],
        scratch_shapes=[
            pltpu.VMEM((9, 2, rows + 2 * EDGE, LANES), jnp.float32),
            pltpu.VMEM((9, 2, rows, LANES), jnp.float32),
        ],
        compiler_params=PARAMS,
        cost_estimate=cost(20_000_000),
    )(ids, kernels, amplitudes, shapes, images, variances, masks)


HALO_SCRATCH = [
    pltpu.VMEM((9, 2, 2 * EDGE, LANES), jnp.float32),
    pltpu.VMEM((9, 2, EDGE, LANES), jnp.float32),
]


def low_part(rows, low, taps, coefs):
    return pl.pallas_call(
        functools.partial(low_kernel, rows),
        in_specs=[VMEM] * 3,
        out_specs=VMEM,
        out_shape=f32(4, EDGE, LANES),
        scratch_shapes=HALO_SCRATCH,
        compiler_params=PARAMS,
        cost_estimate=cost(4_000_000),
    )(low, taps, coefs)


def weighted(own, first, high, taps, coefs):
    rows = own.shape[1]
    return pl.pallas_call(
        weight_kernel,
        in_specs=[VMEM] * 5,
        out_specs=VMEM,
        out_shape=f32(4 * rows, LANES),
        scratch_shapes=HALO_SCRATCH + [pltpu.VMEM((4, EDGE, LANES), jnp.float32)],
        compiler_params=PARAMS,
    )(own, first, high, taps, coefs)


def owned(moved, width):
    return pl.pallas_call(
        owner_kernel,
        in_specs=[VMEM],
        out_specs=[VMEM, VMEM],
        out_shape=[f32(1, width)] * 2,
        compiler_params=PARAMS,
    )(moved)


def before_exchange(images, variances, masks, visit_ids, kernels, amplitudes, shapes):
    strips = lax.axis_size("strip")
    rows = images.shape[1]
    *tables, bottom, top = loaded(
        jnp.transpose(kernels, (1, 3, 2, 0)),
        jnp.transpose(amplitudes, (1, 0)),
        jnp.transpose(shapes, (2, 1, 0)),
        images,
        variances,
    )
    low = lax.ppermute(bottom, "strip", [(i, i + 1) for i in range(strips - 1)])
    high = lax.ppermute(top, "strip", [(i + 1, i) for i in range(strips - 1)])
    own, taps, coefs = strip_parts(visit_ids, *tables, images, variances, masks)
    first = low_part(rows, low, taps, coefs)
    return weighted(own, first, high, taps, coefs)


def shards(images, variances, masks, visit_ids, kernels, amplitudes, shapes):
    rows, width = images.shape[1:]
    visits = lax.axis_size("visit")
    sent = before_exchange(images, variances, masks, visit_ids, kernels, amplitudes, shapes)
    moved = lax.all_to_all(
        sent.reshape(rows, 4, LANES), "visit", split_axis=0, concat_axis=0, tiled=True
    )
    coadd, depth = owned(moved.reshape(visits * 4, LANES), width)
    return coadd, depth


def solution(mesh):
    in_specs = (
        P("visit", "strip", None),
        P("visit", "strip", None),
        P("visit", "strip", None),
        P("visit"),
        P(),
        P(),
        P(),
    )
    out_specs = (P(("strip", "visit"), None), P(("strip", "visit"), None))
    return jax.shard_map(shards, mesh=mesh, in_specs=in_specs, out_specs=out_specs, check_vma=False)
```

```python
import functools

import jax
import jax.numpy as jnp
from jax import lax
from jax.experimental import pallas as pl
from jax.experimental.pallas import tpu as pltpu
from jax.sharding import PartitionSpec as P

pair_first = (0, 1, 2, 0, 0, 1)
pair_second = (0, 1, 2, 1, 2, 2)
pair_count = (1.0, 1.0, 1.0, 2.0, 2.0, 2.0)

LANES = 128
EDGE = 16
VMEM_LIMIT = 32 * 1024 * 1024


def shifted_halves(left, right, shift):
    if shift == 0:
        return left, right
    lane = lax.broadcasted_iota(jnp.int32, left.shape, 1)
    turned_left = pltpu.roll(left, (-shift) % LANES, 1)
    turned_right = pltpu.roll(right, (-shift) % LANES, 1)
    zero = jnp.zeros_like(left)
    if shift > 0:
        inside = lane < LANES - shift
        return jnp.where(inside, turned_left, turned_right), jnp.where(inside, turned_right, zero)
    inside = lane >= -shift
    return jnp.where(inside, turned_left, zero), jnp.where(inside, turned_right, turned_left)


def add_terms(sums, terms):
    return terms if sums is None else [s + t for s, t in zip(sums, terms)]


def columns(images, variances, taps, source, across, target, count):
    span = taps.shape[1]
    for field, maps, base in ((images, 3, 0), (variances, 6, 3)):
        left = field[pl.ds(source, count), 0:LANES]
        right = field[pl.ds(source, count), LANES:]
        sums = None
        for a in range(span):
            moved = shifted_halves(left, right, a - span // 2)
            terms = []
            for j in range(base, base + maps):
                tap = taps[j, a, pl.ds(1, 1), :]
                terms += [tap * m for m in moved]
            sums = add_terms(sums, terms)
        for j in range(maps):
            for side in range(2):
                across[base + j, side, pl.ds(target, count), :] = sums[2 * j + side]


def row_sums(across, taps, down, tiles, offsets):
    tile = 8
    uses = {}
    for t in range(tiles):
        for a, offset in offsets:
            uses.setdefault(tile * t + offset, []).append((t, a))

    def one_map(j, carry):
        tap = {a: taps[j, a, pl.ds(0, 1), :] for a, offset in offsets}
        sums = [[None] * tiles for side in range(2)]
        for place in sorted(uses):
            for side in range(2):
                rows = across[j, side, pl.ds(place, tile), :]
                for t, a in uses[place]:
                    term = tap[a] * rows
                    sums[side][t] = term if sums[side][t] is None else sums[side][t] + term
        for side in range(2):
            for t in range(tiles):
                down[j, side, tile * t : tile * (t + 1), :] = sums[side][t]
        return carry

    lax.fori_loop(0, 9, one_map, 0, unroll=3)


def combine(down, start, count, coefs, row, height, width, store):
    y = (2 * row + 1).astype(jnp.float32) / height - 1.0
    for side in range(2):
        sums = [down[j, side, pl.ds(start, count), :] for j in range(9)]
        basis, paired = sums[:3], sums[3:]
        col = lax.broadcasted_iota(jnp.int32, (count, LANES), 1) + side * LANES
        x = (2 * col + 1).astype(jnp.float32) / width - 1.0
        xx, xy, yy = x * x, x * y, y * y
        factor = []
        for j in range(3):
            s = [coefs[pl.ds(3 * t + j, 1), :] for t in range(6)]
            terms = 1.0 + s[0] * x + s[1] * y
            terms = terms + s[2] * xx + s[3] * xy
            terms = terms + s[4] * yy
            factor.append(s[5] * terms)
        matched = factor[0] * basis[0]
        for j in range(1, 3):
            matched = matched + factor[j] * basis[j]
        spread = None
        for p in range(6):
            cross = factor[pair_first[p]]
            if pair_count[p] != 1.0:
                cross = pair_count[p] * cross
            term = cross * factor[pair_second[p]] * paired[p]
            spread = term if spread is None else spread + term
        store(side, matched, spread)


def of_visit(visit, table):
    here = lax.broadcasted_iota(jnp.int32, table.shape, table.ndim - 1) == visit
    value = jnp.sum(jnp.where(here, table, 0.0), axis=-1, keepdims=True)
    return jnp.broadcast_to(value, table.shape[:-1] + (LANES,))


def strip_is_even():
    return lax.rem(lax.axis_index("strip"), 2) == 0


def load_kernel(
    kernels, amplitudes, shapes, images, variances,
    tap_table, amplitude_table, shape_table, sent_first, sent_second, sems,
):
    rows = images.shape[1]
    place = pl.multiple_of(jnp.where(strip_is_even(), rows - EDGE, 0), EDGE)
    other = pl.multiple_of(jnp.where(strip_is_even(), 0, rows - EDGE), EDGE)
    copies = [
        (images.at[0, pl.ds(place, EDGE)], sent_first.at[0]),
        (variances.at[0, pl.ds(place, EDGE)], sent_first.at[1]),
        (images.at[0, pl.ds(other, EDGE)], sent_second.at[0]),
        (variances.at[0, pl.ds(other, EDGE)], sent_second.at[1]),
        (kernels, tap_table),
        (amplitudes, amplitude_table),
        (shapes, shape_table),
    ]
    copies = [pltpu.make_async_copy(a, b, sems.at[i]) for i, (a, b) in enumerate(copies)]
    for copy in copies:
        copy.start()
    for copy in copies:
        copy.wait()


def strip_kernel(
    ids, tap_table, amplitude_table, shape_table, images, variances, masks,
    out, taps, coefs, across, down,
):
    rows, width = images.shape[1:]
    span = taps.shape[1]
    half = span // 2
    strip_row = lax.axis_index("strip") * rows
    height = rows * lax.axis_size("strip")
    zero = jnp.zeros((9, 2, EDGE, LANES), jnp.float32)
    across[:, :, 0:EDGE] = zero
    across[:, :, rows + EDGE :] = zero

    visit = ids[0]
    taps[0:3] = of_visit(visit, tap_table[...])
    for p, (i, j) in enumerate(zip(pair_first, pair_second)):
        taps[3 + p] = taps[i] * taps[j]
    for t in range(5):
        coefs[3 * t : 3 * t + 3] = of_visit(visit, shape_table[t])
    coefs[15:18] = of_visit(visit, amplitude_table[...])

    chunk = 32

    def inner(step, carry):
        start = pl.multiple_of(step * chunk, chunk)
        columns(images.at[0], variances.at[0], taps, start, across, start + EDGE, chunk)
        return carry

    lax.fori_loop(0, rows // chunk, inner, 0)
    row_sums(across, taps, down, rows // 8, [(a, EDGE - half + a) for a in range(span)])

    block = 32
    for start in range(0, rows, block):
        row = lax.broadcasted_iota(jnp.int32, (block, LANES), 0) + (start + strip_row)

        def store(side, matched, spread):
            mask = masks[0, pl.ds(start, block), side * LANES : (side + 1) * LANES]
            valid = jnp.bitwise_and(mask, 7) == 0
            out[side, pl.ds(start, block), :] = matched
            out[2 + side, pl.ds(start, block), :] = jnp.where(valid, spread, jnp.inf)

        combine(down, start, block, coefs, row, height, width, store)


def halo_part(halo, after, taps, coefs, padded, down, rows, store):
    span = taps.shape[1]
    half = span // 2
    zero = jnp.zeros((9, 2, EDGE, LANES), jnp.float32)
    padded[:, :, 0:EDGE] = zero
    padded[:, :, 2 * EDGE :] = zero
    columns(halo.at[0], halo.at[1], taps, 0, padded, EDGE, EDGE)

    @pl.when(after)
    def _():
        row_sums(padded, taps, down, EDGE // 8, [(a, a - half) for a in range(half + 1, span)])

    @pl.when(jnp.logical_not(after))
    def _():
        row_sums(padded, taps, down, EDGE // 8, [(a, 2 * EDGE - half + a) for a in range(half)])

    first_row = lax.axis_index("strip") * rows + jnp.where(after, rows - EDGE, 0)
    row = lax.broadcasted_iota(jnp.int32, (EDGE, LANES), 0) + first_row
    height = rows * lax.axis_size("strip")
    combine(down, 0, EDGE, coefs, row, height, halo.shape[2], store)


def first_kernel(rows, halo, taps, coefs, out, padded, down):
    def store(side, matched, spread):
        out[side] = matched
        out[2 + side] = spread

    halo_part(halo, strip_is_even(), taps, coefs, padded, down, rows, store)


def weight_kernel(own, first, halo, taps, coefs, out, padded, down, second):
    rows = own.shape[1]
    even = strip_is_even()

    def store(side, matched, spread):
        second[side] = matched
        second[2 + side] = spread

    halo_part(halo, jnp.logical_not(even), taps, coefs, padded, down, rows, store)
    for extra, start in (
        (first, jnp.where(even, rows - EDGE, 0)),
        (None, EDGE),
        (second, jnp.where(even, 0, rows - EDGE)),
    ):
        count = EDGE if extra is not None else rows - 2 * EDGE
        start = pl.multiple_of(start, EDGE) if extra is not None else start
        for side in range(2):
            matched = own[side, pl.ds(start, count), :]
            spread = own[2 + side, pl.ds(start, count), :]
            if extra is not None:
                matched = matched + extra[side]
                spread = spread + extra[2 + side]
            out[pl.ds(4 * start + side, count, stride=4), :] = matched
            out[pl.ds(4 * start + 2 + side, count, stride=4), :] = 1.0 / spread


def owner_kernel(moved, coadd, depth):
    visits = moved.shape[0] // 4
    for side in range(2):
        matched = moved[pl.ds(side, visits, stride=4), :]
        weight = moved[pl.ds(2 + side, visits, stride=4), :]
        valid = weight > 0.0
        visit = lax.broadcasted_iota(jnp.int32, matched.shape, 0)

        def extreme(values, value):
            first = jnp.min(jnp.where(values == value, visit, visits), axis=0, keepdims=True)
            return jnp.sum(jnp.where(visit == first, weight, 0.0), axis=0, keepdims=True)

        low_values = jnp.where(valid, matched, jnp.inf)
        high_values = jnp.where(valid, matched, -jnp.inf)
        low_value = jnp.min(low_values, axis=0, keepdims=True)
        high_value = jnp.max(high_values, axis=0, keepdims=True)
        low_weight = extreme(low_values, low_value)
        high_weight = extreme(high_values, high_value)
        total = jnp.sum(weight * matched, axis=0, keepdims=True)
        weights = jnp.sum(weight, axis=0, keepdims=True)
        lanes = slice(side * LANES, (side + 1) * LANES)
        coadd[:, lanes] = (total - low_weight * low_value - high_weight * high_value) / (
            weights - low_weight - high_weight
        )
        depth[:, lanes] = jnp.log(weights + 1.0)


VMEM = pl.BlockSpec(memory_space=pltpu.VMEM)
HBM = pl.BlockSpec(memory_space=pltpu.HBM)
SMEM = pl.BlockSpec(memory_space=pltpu.SMEM)
PARAMS = pltpu.CompilerParams(vmem_limit_bytes=VMEM_LIMIT)


def f32(*shape):
    return jax.ShapeDtypeStruct(shape, jnp.float32)


def cost(flops):
    return pl.CostEstimate(flops=flops, bytes_accessed=1 << 20, transcendentals=0)


def loaded(kernels, amplitudes, shapes, images, variances):
    width = images.shape[2]
    return pl.pallas_call(
        load_kernel,
        in_specs=[HBM] * 5,
        out_specs=[VMEM] * 5,
        out_shape=[
            f32(*kernels.shape),
            f32(*amplitudes.shape),
            f32(*shapes.shape),
            f32(2, EDGE, width),
            f32(2, EDGE, width),
        ],
        scratch_shapes=[pltpu.SemaphoreType.DMA((7,))],
        compiler_params=PARAMS,
    )(
        *(
            pltpu.with_memory_space_constraint(x, pltpu.HBM)
            for x in (kernels, amplitudes, shapes, images, variances)
        )
    )


def strip_parts(ids, kernels, amplitudes, shapes, images, variances, masks):
    rows = images.shape[1]
    return pl.pallas_call(
        strip_kernel,
        in_specs=[SMEM] + [VMEM] * 6,
        out_specs=[VMEM] * 3,
        out_shape=[f32(4, rows, LANES), f32(9, *kernels.shape[1:3], LANES), f32(18, LANES)],
        scratch_shapes=[
            pltpu.VMEM((9, 2, rows + 2 * EDGE, LANES), jnp.float32),
            pltpu.VMEM((9, 2, rows, LANES), jnp.float32),
        ],
        compiler_params=PARAMS,
        cost_estimate=cost(20_000_000),
    )(ids, kernels, amplitudes, shapes, images, variances, masks)


HALO_SCRATCH = [
    pltpu.VMEM((9, 2, 3 * EDGE, LANES), jnp.float32),
    pltpu.VMEM((9, 2, EDGE, LANES), jnp.float32),
]


def first_part(rows, halo, taps, coefs):
    return pl.pallas_call(
        functools.partial(first_kernel, rows),
        in_specs=[VMEM] * 3,
        out_specs=VMEM,
        out_shape=f32(4, EDGE, LANES),
        scratch_shapes=HALO_SCRATCH,
        compiler_params=PARAMS,
        cost_estimate=cost(4_000_000),
    )(halo, taps, coefs)


def weighted(own, first, halo, taps, coefs):
    rows = own.shape[1]
    return pl.pallas_call(
        weight_kernel,
        in_specs=[VMEM] * 5,
        out_specs=VMEM,
        out_shape=f32(4 * rows, LANES),
        scratch_shapes=HALO_SCRATCH + [pltpu.VMEM((4, EDGE, LANES), jnp.float32)],
        compiler_params=PARAMS,
    )(own, first, halo, taps, coefs)


def owned(moved, width):
    return pl.pallas_call(
        owner_kernel,
        in_specs=[VMEM],
        out_specs=[VMEM, VMEM],
        out_shape=[f32(1, width)] * 2,
        compiler_params=PARAMS,
    )(moved)


def before_exchange(images, variances, masks, visit_ids, kernels, amplitudes, shapes):
    strips = lax.axis_size("strip")
    rows = images.shape[1]
    *tables, sent_first, sent_second = loaded(
        jnp.transpose(kernels, (1, 3, 2, 0)),
        jnp.transpose(amplitudes, (1, 0)),
        jnp.transpose(shapes, (2, 1, 0)),
        images,
        variances,
    )

    def swap(edge, start):
        pairs = [(i, i + 1) for i in range(start, strips - 1, 2)]
        return lax.ppermute(edge, "strip", pairs + [(b, a) for a, b in pairs])

    halo_first = swap(sent_first, 0)
    halo_second = swap(sent_second, 1)
    own, taps, coefs = strip_parts(visit_ids, *tables, images, variances, masks)
    first = first_part(rows, halo_first, taps, coefs)
    return weighted(own, first, halo_second, taps, coefs)


def shards(images, variances, masks, visit_ids, kernels, amplitudes, shapes):
    rows, width = images.shape[1:]
    visits = lax.axis_size("visit")
    sent = before_exchange(images, variances, masks, visit_ids, kernels, amplitudes, shapes)
    moved = lax.all_to_all(
        sent.reshape(rows, 4, LANES), "visit", split_axis=0, concat_axis=0, tiled=True
    )
    coadd, depth = owned(moved.reshape(visits * 4, LANES), width)
    return coadd, depth


def solution(mesh):
    in_specs = (
        P("visit", "strip", None),
        P("visit", "strip", None),
        P("visit", "strip", None),
        P("visit"),
        P(),
        P(),
        P(),
    )
    out_specs = (P(("strip", "visit"), None), P(("strip", "visit"), None))
    return jax.shard_map(shards, mesh=mesh, in_specs=in_specs, out_specs=out_specs, check_vma=False)
```

```python
import functools

import jax
import jax.numpy as jnp
from jax import lax
from jax.experimental import pallas as pl
from jax.experimental.pallas import tpu as pltpu
from jax.sharding import PartitionSpec as P

pair_first = (0, 1, 2, 0, 0, 1)
pair_second = (0, 1, 2, 1, 2, 2)
pair_count = (1.0, 1.0, 1.0, 2.0, 2.0, 2.0)

LANES = 128
EDGE = 16
VMEM_LIMIT = 32 * 1024 * 1024


def shifted_halves(left, right, shift):
    if shift == 0:
        return left, right
    lane = lax.broadcasted_iota(jnp.int32, left.shape, 1)
    turned_left = pltpu.roll(left, (-shift) % LANES, 1)
    turned_right = pltpu.roll(right, (-shift) % LANES, 1)
    zero = jnp.zeros_like(left)
    if shift > 0:
        inside = lane < LANES - shift
        return jnp.where(inside, turned_left, turned_right), jnp.where(inside, turned_right, zero)
    inside = lane >= -shift
    return jnp.where(inside, turned_left, zero), jnp.where(inside, turned_right, turned_left)


def add_terms(sums, terms):
    return terms if sums is None else [s + t for s, t in zip(sums, terms)]


def columns(fields, taps, source, across, target, count):
    span = taps.shape[1]
    for field, maps, base in fields:
        left = field[pl.ds(source, count), 0:LANES]
        right = field[pl.ds(source, count), LANES:]
        sums = None
        for a in range(span):
            moved = shifted_halves(left, right, a - span // 2)
            terms = []
            for j in range(base, base + maps):
                tap = taps[j, a, pl.ds(1, 1), :]
                terms += [tap * m for m in moved]
            sums = add_terms(sums, terms)
        for j in range(maps):
            for side in range(2):
                across[base + j, side, pl.ds(target, count), :] = sums[2 * j + side]


def row_sums(across, taps, down, tiles, offsets, maps=9):
    tile = 8
    uses = {}
    for t in range(tiles):
        for a, offset in offsets:
            uses.setdefault(tile * t + offset, []).append((t, a))

    def one_map(j, carry):
        tap = {a: taps[j, a, pl.ds(0, 1), :] for a, offset in offsets}
        sums = [[None] * tiles for side in range(2)]
        for place in sorted(uses):
            for side in range(2):
                rows = across[j, side, pl.ds(place, tile), :]
                for t, a in uses[place]:
                    term = tap[a] * rows
                    sums[side][t] = term if sums[side][t] is None else sums[side][t] + term
        for side in range(2):
            for t in range(tiles):
                down[j, side, tile * t : tile * (t + 1), :] = sums[side][t]
        return carry

    lax.fori_loop(0, maps, one_map, 0, unroll=3)


def combine(down, start, count, coefs, row, height, width, store):
    y = (2 * row + 1).astype(jnp.float32) / height - 1.0
    for side in range(2):
        sums = [down[j, side, pl.ds(start, count), :] for j in range(9)]
        basis, paired = sums[:3], sums[3:]
        col = lax.broadcasted_iota(jnp.int32, (count, LANES), 1) + side * LANES
        x = (2 * col + 1).astype(jnp.float32) / width - 1.0
        xx, xy, yy = x * x, x * y, y * y
        factor = []
        for j in range(3):
            s = [coefs[pl.ds(3 * t + j, 1), :] for t in range(6)]
            terms = 1.0 + s[0] * x + s[1] * y
            terms = terms + s[2] * xx + s[3] * xy
            terms = terms + s[4] * yy
            factor.append(s[5] * terms)
        matched = factor[0] * basis[0]
        for j in range(1, 3):
            matched = matched + factor[j] * basis[j]
        spread = None
        for p in range(6):
            cross = factor[pair_first[p]]
            if pair_count[p] != 1.0:
                cross = pair_count[p] * cross
            term = cross * factor[pair_second[p]] * paired[p]
            spread = term if spread is None else spread + term
        store(side, matched, spread)


def of_visit(visit, table):
    here = lax.broadcasted_iota(jnp.int32, table.shape, table.ndim - 1) == visit
    value = jnp.sum(jnp.where(here, table, 0.0), axis=-1, keepdims=True)
    return jnp.broadcast_to(value, table.shape[:-1] + (LANES,))


def two_parts(x):
    high = x.astype(jnp.bfloat16)
    return high, (x - high.astype(jnp.float32)).astype(jnp.bfloat16)


def product(left, right):
    count = left.shape[0]
    left_high, left_low = two_parts(left)
    right_high, right_low = right
    both = jnp.dot(
        jnp.concatenate([left_high, left_low]), right_high, preferred_element_type=jnp.float32
    )
    cross = jnp.dot(left_high, right_low, preferred_element_type=jnp.float32)
    return both[:count] + (both[count:] + cross)


def band(taps, j, kind, count, sign):
    span = taps.shape[1]
    half = span // 2
    lane = lax.broadcasted_iota(jnp.int32, (1, LANES), 1)
    line = jnp.zeros((1, LANES), jnp.float32)
    for a in range(span):
        line = jnp.where(lane == sign * (a - half) % LANES, taps[j, a, pl.ds(kind, 1), :], line)
    line = jnp.broadcast_to(line, (count, LANES))
    return pltpu.roll(line, 0, 1, stride=1, stride_axis=0)


def variance_maps(variances, taps, down):
    rows = variances.shape[1]
    half = taps.shape[1] // 2
    row = lax.broadcasted_iota(jnp.int32, (rows, LANES), 0)
    lane = lax.broadcasted_iota(jnp.int32, (rows, LANES), 1)
    near = jnp.logical_and(jnp.abs(lane - row) <= half, lane < rows)
    row_bands = jnp.concatenate(
        [jnp.where(near, band(taps, 3 + p, 0, rows, 1), 0.0)[:, :rows] for p in range(6)]
    )
    sums = product(row_bands, two_parts(variances[0]))
    apart = lax.broadcasted_iota(jnp.int32, (LANES, LANES), 1) - lax.broadcasted_iota(
        jnp.int32, (LANES, LANES), 0
    )
    for p in range(6):
        ring = band(taps, 3 + p, 1, LANES, -1)
        inner = jnp.where(jnp.abs(apart) <= half, ring, 0.0)
        after = jnp.where(apart < -half, ring, 0.0)
        before = jnp.where(apart > half, ring, 0.0)
        column_band = jnp.concatenate(
            [jnp.concatenate([inner, after], axis=1), jnp.concatenate([before, inner], axis=1)]
        )
        result = product(sums[p * rows : (p + 1) * rows], two_parts(column_band))
        for side in range(2):
            down[3 + p, side] = result[:, side * LANES : (side + 1) * LANES]


def strip_is_even():
    return lax.rem(lax.axis_index("strip"), 2) == 0


def load_kernel(
    kernels, amplitudes, shapes, images, variances,
    tap_table, amplitude_table, shape_table, sent_first, sent_second, sems,
):
    rows = images.shape[1]
    place = pl.multiple_of(jnp.where(strip_is_even(), rows - EDGE, 0), EDGE)
    other = pl.multiple_of(jnp.where(strip_is_even(), 0, rows - EDGE), EDGE)
    copies = [
        (images.at[0, pl.ds(place, EDGE)], sent_first.at[0]),
        (variances.at[0, pl.ds(place, EDGE)], sent_first.at[1]),
        (images.at[0, pl.ds(other, EDGE)], sent_second.at[0]),
        (variances.at[0, pl.ds(other, EDGE)], sent_second.at[1]),
        (kernels, tap_table),
        (amplitudes, amplitude_table),
        (shapes, shape_table),
    ]
    copies = [pltpu.make_async_copy(a, b, sems.at[i]) for i, (a, b) in enumerate(copies)]
    for copy in copies:
        copy.start()
    for copy in copies:
        copy.wait()


def strip_kernel(
    ids, tap_table, amplitude_table, shape_table, images, variances, masks,
    out, taps, coefs, across, down,
):
    rows, width = images.shape[1:]
    span = taps.shape[1]
    half = span // 2
    strip_row = lax.axis_index("strip") * rows
    height = rows * lax.axis_size("strip")
    zero = jnp.zeros((3, 2, EDGE, LANES), jnp.float32)
    across[:, :, 0:EDGE] = zero
    across[:, :, rows + EDGE :] = zero

    visit = ids[0]
    taps[0:3] = of_visit(visit, tap_table[...])
    for p, (i, j) in enumerate(zip(pair_first, pair_second)):
        taps[3 + p] = taps[i] * taps[j]
    for t in range(5):
        coefs[3 * t : 3 * t + 3] = of_visit(visit, shape_table[t])
    coefs[15:18] = of_visit(visit, amplitude_table[...])

    chunk = 32

    def inner(step, carry):
        start = pl.multiple_of(step * chunk, chunk)
        columns(((images.at[0], 3, 0),), taps, start, across, start + EDGE, chunk)
        return carry

    lax.fori_loop(0, rows // chunk, inner, 0)
    row_sums(across, taps, down, rows // 8, [(a, EDGE - half + a) for a in range(span)], maps=3)
    variance_maps(variances, taps, down)

    block = 32
    for start in range(0, rows, block):
        row = lax.broadcasted_iota(jnp.int32, (block, LANES), 0) + (start + strip_row)

        def store(side, matched, spread):
            mask = masks[0, pl.ds(start, block), side * LANES : (side + 1) * LANES]
            valid = jnp.bitwise_and(mask, 7) == 0
            out[side, pl.ds(start, block), :] = matched
            out[2 + side, pl.ds(start, block), :] = jnp.where(valid, spread, jnp.inf)

        combine(down, start, block, coefs, row, height, width, store)


def halo_part(halo, after, taps, coefs, padded, down, rows, store):
    span = taps.shape[1]
    half = span // 2
    zero = jnp.zeros((9, 2, EDGE, LANES), jnp.float32)
    padded[:, :, 0:EDGE] = zero
    padded[:, :, 2 * EDGE :] = zero
    columns(((halo.at[0], 3, 0), (halo.at[1], 6, 3)), taps, 0, padded, EDGE, EDGE)

    @pl.when(after)
    def _():
        row_sums(padded, taps, down, EDGE // 8, [(a, a - half) for a in range(half + 1, span)])

    @pl.when(jnp.logical_not(after))
    def _():
        row_sums(padded, taps, down, EDGE // 8, [(a, 2 * EDGE - half + a) for a in range(half)])

    first_row = lax.axis_index("strip") * rows + jnp.where(after, rows - EDGE, 0)
    row = lax.broadcasted_iota(jnp.int32, (EDGE, LANES), 0) + first_row
    height = rows * lax.axis_size("strip")
    combine(down, 0, EDGE, coefs, row, height, halo.shape[2], store)


def first_kernel(rows, halo, taps, coefs, out, padded, down):
    def store(side, matched, spread):
        out[side] = matched
        out[2 + side] = spread

    halo_part(halo, strip_is_even(), taps, coefs, padded, down, rows, store)


def weight_kernel(own, first, halo, taps, coefs, out, padded, down, second):
    rows = own.shape[1]
    even = strip_is_even()

    def store(side, matched, spread):
        second[side] = matched
        second[2 + side] = spread

    halo_part(halo, jnp.logical_not(even), taps, coefs, padded, down, rows, store)
    for extra, start in (
        (first, jnp.where(even, rows - EDGE, 0)),
        (None, EDGE),
        (second, jnp.where(even, 0, rows - EDGE)),
    ):
        count = EDGE if extra is not None else rows - 2 * EDGE
        start = pl.multiple_of(start, EDGE) if extra is not None else start
        for side in range(2):
            matched = own[side, pl.ds(start, count), :]
            spread = own[2 + side, pl.ds(start, count), :]
            if extra is not None:
                matched = matched + extra[side]
                spread = spread + extra[2 + side]
            out[pl.ds(4 * start + side, count, stride=4), :] = matched
            out[pl.ds(4 * start + 2 + side, count, stride=4), :] = 1.0 / spread


def owner_kernel(moved, coadd, depth):
    visits = moved.shape[0] // 4
    for side in range(2):
        matched = moved[pl.ds(side, visits, stride=4), :]
        weight = moved[pl.ds(2 + side, visits, stride=4), :]
        valid = weight > 0.0
        visit = lax.broadcasted_iota(jnp.int32, matched.shape, 0)

        def extreme(values, value):
            first = jnp.min(jnp.where(values == value, visit, visits), axis=0, keepdims=True)
            return jnp.sum(jnp.where(visit == first, weight, 0.0), axis=0, keepdims=True)

        low_values = jnp.where(valid, matched, jnp.inf)
        high_values = jnp.where(valid, matched, -jnp.inf)
        low_value = jnp.min(low_values, axis=0, keepdims=True)
        high_value = jnp.max(high_values, axis=0, keepdims=True)
        low_weight = extreme(low_values, low_value)
        high_weight = extreme(high_values, high_value)
        total = jnp.sum(weight * matched, axis=0, keepdims=True)
        weights = jnp.sum(weight, axis=0, keepdims=True)
        lanes = slice(side * LANES, (side + 1) * LANES)
        coadd[:, lanes] = (total - low_weight * low_value - high_weight * high_value) / (
            weights - low_weight - high_weight
        )
        depth[:, lanes] = jnp.log(weights + 1.0)


VMEM = pl.BlockSpec(memory_space=pltpu.VMEM)
HBM = pl.BlockSpec(memory_space=pltpu.HBM)
SMEM = pl.BlockSpec(memory_space=pltpu.SMEM)
PARAMS = pltpu.CompilerParams(vmem_limit_bytes=VMEM_LIMIT)


def f32(*shape):
    return jax.ShapeDtypeStruct(shape, jnp.float32)


def cost(flops):
    return pl.CostEstimate(flops=flops, bytes_accessed=1 << 20, transcendentals=0)


def loaded(kernels, amplitudes, shapes, images, variances):
    width = images.shape[2]
    return pl.pallas_call(
        load_kernel,
        in_specs=[HBM] * 5,
        out_specs=[VMEM] * 5,
        out_shape=[
            f32(*kernels.shape),
            f32(*amplitudes.shape),
            f32(*shapes.shape),
            f32(2, EDGE, width),
            f32(2, EDGE, width),
        ],
        scratch_shapes=[pltpu.SemaphoreType.DMA((7,))],
        compiler_params=PARAMS,
    )(
        *(
            pltpu.with_memory_space_constraint(x, pltpu.HBM)
            for x in (kernels, amplitudes, shapes, images, variances)
        )
    )


def strip_parts(ids, kernels, amplitudes, shapes, images, variances, masks):
    rows = images.shape[1]
    return pl.pallas_call(
        strip_kernel,
        in_specs=[SMEM] + [VMEM] * 6,
        out_specs=[VMEM] * 3,
        out_shape=[f32(4, rows, LANES), f32(9, *kernels.shape[1:3], LANES), f32(18, LANES)],
        scratch_shapes=[
            pltpu.VMEM((3, 2, rows + 2 * EDGE, LANES), jnp.float32),
            pltpu.VMEM((9, 2, rows, LANES), jnp.float32),
        ],
        compiler_params=PARAMS,
        cost_estimate=cost(20_000_000),
    )(ids, kernels, amplitudes, shapes, images, variances, masks)


HALO_SCRATCH = [
    pltpu.VMEM((9, 2, 3 * EDGE, LANES), jnp.float32),
    pltpu.VMEM((9, 2, EDGE, LANES), jnp.float32),
]


def first_part(rows, halo, taps, coefs):
    return pl.pallas_call(
        functools.partial(first_kernel, rows),
        in_specs=[VMEM] * 3,
        out_specs=VMEM,
        out_shape=f32(4, EDGE, LANES),
        scratch_shapes=HALO_SCRATCH,
        compiler_params=PARAMS,
        cost_estimate=cost(4_000_000),
    )(halo, taps, coefs)


def weighted(own, first, halo, taps, coefs):
    rows = own.shape[1]
    return pl.pallas_call(
        weight_kernel,
        in_specs=[VMEM] * 5,
        out_specs=VMEM,
        out_shape=f32(4 * rows, LANES),
        scratch_shapes=HALO_SCRATCH + [pltpu.VMEM((4, EDGE, LANES), jnp.float32)],
        compiler_params=PARAMS,
    )(own, first, halo, taps, coefs)


def owned(moved, width):
    return pl.pallas_call(
        owner_kernel,
        in_specs=[VMEM],
        out_specs=[VMEM, VMEM],
        out_shape=[f32(1, width)] * 2,
        compiler_params=PARAMS,
    )(moved)


def before_exchange(images, variances, masks, visit_ids, kernels, amplitudes, shapes):
    strips = lax.axis_size("strip")
    rows = images.shape[1]
    *tables, sent_first, sent_second = loaded(
        jnp.transpose(kernels, (1, 3, 2, 0)),
        jnp.transpose(amplitudes, (1, 0)),
        jnp.transpose(shapes, (2, 1, 0)),
        images,
        variances,
    )

    def swap(edge, start):
        pairs = [(i, i + 1) for i in range(start, strips - 1, 2)]
        return lax.ppermute(edge, "strip", pairs + [(b, a) for a, b in pairs])

    halo_first = swap(sent_first, 0)
    halo_second = swap(sent_second, 1)
    own, taps, coefs = strip_parts(visit_ids, *tables, images, variances, masks)
    first = first_part(rows, halo_first, taps, coefs)
    return weighted(own, first, halo_second, taps, coefs)


def shards(images, variances, masks, visit_ids, kernels, amplitudes, shapes):
    rows, width = images.shape[1:]
    visits = lax.axis_size("visit")
    sent = before_exchange(images, variances, masks, visit_ids, kernels, amplitudes, shapes)
    moved = lax.all_to_all(
        sent.reshape(rows, 4, LANES), "visit", split_axis=0, concat_axis=0, tiled=True
    )
    coadd, depth = owned(moved.reshape(visits * 4, LANES), width)
    return coadd, depth


def solution(mesh):
    in_specs = (
        P("visit", "strip", None),
        P("visit", "strip", None),
        P("visit", "strip", None),
        P("visit"),
        P(),
        P(),
        P(),
    )
    out_specs = (P(("strip", "visit"), None), P(("strip", "visit"), None))
    return jax.shard_map(shards, mesh=mesh, in_specs=in_specs, out_specs=out_specs, check_vma=False)
```

```python
import functools

import jax
import jax.numpy as jnp
from jax import lax
from jax.experimental import pallas as pl
from jax.experimental.pallas import tpu as pltpu
from jax.sharding import PartitionSpec as P

pair_first = (0, 1, 2, 0, 0, 1)
pair_second = (0, 1, 2, 1, 2, 2)
pair_count = (1.0, 1.0, 1.0, 2.0, 2.0, 2.0)

LANES = 128
EDGE = 16
VMEM_LIMIT = 32 * 1024 * 1024


def shifted_halves(left, right, shift):
    if shift == 0:
        return left, right
    lane = lax.broadcasted_iota(jnp.int32, left.shape, 1)
    turned_left = pltpu.roll(left, (-shift) % LANES, 1)
    turned_right = pltpu.roll(right, (-shift) % LANES, 1)
    zero = jnp.zeros_like(left)
    if shift > 0:
        inside = lane < LANES - shift
        return jnp.where(inside, turned_left, turned_right), jnp.where(inside, turned_right, zero)
    inside = lane >= -shift
    return jnp.where(inside, turned_left, zero), jnp.where(inside, turned_right, turned_left)


def add_terms(sums, terms):
    return terms if sums is None else [s + t for s, t in zip(sums, terms)]


def columns(fields, taps, source, across, target, count):
    span = taps.shape[1]
    for field, maps, base in fields:
        left = field[pl.ds(source, count), 0:LANES]
        right = field[pl.ds(source, count), LANES:]
        sums = None
        for a in range(span):
            moved = shifted_halves(left, right, a - span // 2)
            terms = []
            for j in range(base, base + maps):
                tap = taps[j, a, pl.ds(1, 1), :]
                terms += [tap * m for m in moved]
            sums = add_terms(sums, terms)
        for j in range(maps):
            for side in range(2):
                across[base + j, side, pl.ds(target, count), :] = sums[2 * j + side]


def row_sums(across, taps, down, tiles, offsets, maps=9):
    tile = 8
    uses = {}
    for t in range(tiles):
        for a, offset in offsets:
            uses.setdefault(tile * t + offset, []).append((t, a))

    def one_map(j, carry):
        tap = {a: taps[j, a, pl.ds(0, 1), :] for a, offset in offsets}
        sums = [[None] * tiles for side in range(2)]
        for place in sorted(uses):
            for side in range(2):
                rows = across[j, side, pl.ds(place, tile), :]
                for t, a in uses[place]:
                    term = tap[a] * rows
                    sums[side][t] = term if sums[side][t] is None else sums[side][t] + term
        for side in range(2):
            for t in range(tiles):
                down[j, side, tile * t : tile * (t + 1), :] = sums[side][t]
        return carry

    lax.fori_loop(0, maps, one_map, 0, unroll=3)


def combine(down, start, count, coefs, row, height, width, store):
    y = (2 * row + 1).astype(jnp.float32) / height - 1.0
    for side in range(2):
        sums = [down[j, side, pl.ds(start, count), :] for j in range(9)]
        basis, paired = sums[:3], sums[3:]
        col = lax.broadcasted_iota(jnp.int32, (count, LANES), 1) + side * LANES
        x = (2 * col + 1).astype(jnp.float32) / width - 1.0
        xx, xy, yy = x * x, x * y, y * y
        factor = []
        for j in range(3):
            s = [coefs[pl.ds(3 * t + j, 1), :] for t in range(6)]
            terms = 1.0 + s[0] * x + s[1] * y
            terms = terms + s[2] * xx + s[3] * xy
            terms = terms + s[4] * yy
            factor.append(s[5] * terms)
        matched = factor[0] * basis[0]
        for j in range(1, 3):
            matched = matched + factor[j] * basis[j]
        spread = None
        for p in range(6):
            cross = factor[pair_first[p]]
            if pair_count[p] != 1.0:
                cross = pair_count[p] * cross
            term = cross * factor[pair_second[p]] * paired[p]
            spread = term if spread is None else spread + term
        store(side, matched, spread)


def of_visit(visit, table):
    here = lax.broadcasted_iota(jnp.int32, table.shape, table.ndim - 1) == visit
    value = jnp.sum(jnp.where(here, table, 0.0), axis=-1, keepdims=True)
    return jnp.broadcast_to(value, table.shape[:-1] + (LANES,))


def two_parts(x):
    high = x.astype(jnp.bfloat16)
    return high, (x - high.astype(jnp.float32)).astype(jnp.bfloat16)


def product(left, right):
    count = left.shape[0]
    left_high, left_low = two_parts(left)
    right_high, right_low = right
    both = jnp.dot(
        jnp.concatenate([left_high, left_low]), right_high, preferred_element_type=jnp.float32
    )
    cross = jnp.dot(left_high, right_low, preferred_element_type=jnp.float32)
    return both[:count] + (both[count:] + cross)


def band(taps, j, kind, count, sign):
    span = taps.shape[1]
    half = span // 2
    lane = lax.broadcasted_iota(jnp.int32, (1, LANES), 1)
    line = jnp.zeros((1, LANES), jnp.float32)
    for a in range(span):
        line = jnp.where(lane == sign * (a - half) % LANES, taps[j, a, pl.ds(kind, 1), :], line)
    line = jnp.broadcast_to(line, (count, LANES))
    return pltpu.roll(line, 0, 1, stride=1, stride_axis=0)


def variance_maps(variances, taps, down):
    rows = variances.shape[1]
    half = taps.shape[1] // 2
    row = lax.broadcasted_iota(jnp.int32, (rows, LANES), 0)
    lane = lax.broadcasted_iota(jnp.int32, (rows, LANES), 1)
    near = jnp.logical_and(jnp.abs(lane - row) <= half, lane < rows)
    row_bands = jnp.concatenate(
        [jnp.where(near, band(taps, 3 + p, 0, rows, 1), 0.0)[:, :rows] for p in range(6)]
    )
    sums = product(row_bands, two_parts(variances[0]))
    apart = lax.broadcasted_iota(jnp.int32, (LANES, LANES), 1) - lax.broadcasted_iota(
        jnp.int32, (LANES, LANES), 0
    )
    for p in range(6):
        ring = band(taps, 3 + p, 1, LANES, -1)
        inner = jnp.where(jnp.abs(apart) <= half, ring, 0.0)
        after = jnp.where(apart < -half, ring, 0.0)
        before = jnp.where(apart > half, ring, 0.0)
        column_band = jnp.concatenate(
            [jnp.concatenate([inner, after], axis=1), jnp.concatenate([before, inner], axis=1)]
        )
        result = product(sums[p * rows : (p + 1) * rows], two_parts(column_band))
        for side in range(2):
            down[3 + p, side] = result[:, side * LANES : (side + 1) * LANES]


def strip_is_even():
    return lax.rem(lax.axis_index("strip"), 2) == 0


def load_kernel(images, variances, image_rows, variance_rows, sent_first, sent_second, sems):
    rows = images.shape[1]
    copies = [
        pltpu.make_async_copy(images, image_rows, sems.at[0]),
        pltpu.make_async_copy(variances, variance_rows, sems.at[1]),
    ]
    for copy in copies:
        copy.start()
    place = pl.multiple_of(jnp.where(strip_is_even(), rows - EDGE, 0), EDGE)
    other = pl.multiple_of(jnp.where(strip_is_even(), 0, rows - EDGE), EDGE)
    for i, field in enumerate((image_rows, variance_rows)):
        copies[i].wait()
        sent_first[i] = field[0, pl.ds(place, EDGE)]
        sent_second[i] = field[0, pl.ds(other, EDGE)]


def strip_kernel(
    ids, tap_table, amplitudes, shapes, images, variances, masks,
    out, taps, coefs, across, down, amplitude_table, shape_table, mask, sems,
):
    rows, width = images.shape[1:]
    span = taps.shape[1]
    half = span // 2
    strip_row = lax.axis_index("strip") * rows
    height = rows * lax.axis_size("strip")
    copies = [(amplitudes, amplitude_table), (shapes, shape_table), (masks, mask)]
    copies = [pltpu.make_async_copy(a, b, sems.at[i]) for i, (a, b) in enumerate(copies)]
    for copy in copies:
        copy.start()
    zero = jnp.zeros((3, 2, EDGE, LANES), jnp.float32)
    across[:, :, 0:EDGE] = zero
    across[:, :, rows + EDGE :] = zero

    visit = ids[0]
    taps[0:3] = of_visit(visit, tap_table[...])
    for p, (i, j) in enumerate(zip(pair_first, pair_second)):
        taps[3 + p] = taps[i] * taps[j]
    chunk = 32

    def inner(step, carry):
        start = pl.multiple_of(step * chunk, chunk)
        columns(((images.at[0], 3, 0),), taps, start, across, start + EDGE, chunk)
        return carry

    lax.fori_loop(0, rows // chunk, inner, 0)
    row_sums(across, taps, down, rows // 8, [(a, EDGE - half + a) for a in range(span)], maps=3)
    for copy in copies:
        copy.wait()
    for t in range(5):
        coefs[3 * t : 3 * t + 3] = of_visit(visit, shape_table[t])
    coefs[15:18] = of_visit(visit, amplitude_table[...])
    variance_maps(variances, taps, down)

    block = 32
    for start in range(0, rows, block):
        row = lax.broadcasted_iota(jnp.int32, (block, LANES), 0) + (start + strip_row)

        def store(side, matched, spread):
            bits = mask[0, pl.ds(start, block), side * LANES : (side + 1) * LANES]
            valid = jnp.bitwise_and(bits, 7) == 0
            out[side, pl.ds(start, block), :] = matched
            out[2 + side, pl.ds(start, block), :] = jnp.where(valid, spread, jnp.inf)

        combine(down, start, block, coefs, row, height, width, store)


def halo_part(halo, after, taps, coefs, padded, down, rows, store):
    span = taps.shape[1]
    half = span // 2
    zero = jnp.zeros((9, 2, EDGE, LANES), jnp.float32)
    padded[:, :, 0:EDGE] = zero
    padded[:, :, 2 * EDGE :] = zero
    columns(((halo.at[0], 3, 0), (halo.at[1], 6, 3)), taps, 0, padded, EDGE, EDGE)

    @pl.when(after)
    def _():
        row_sums(padded, taps, down, EDGE // 8, [(a, a - half) for a in range(half + 1, span)])

    @pl.when(jnp.logical_not(after))
    def _():
        row_sums(padded, taps, down, EDGE // 8, [(a, 2 * EDGE - half + a) for a in range(half)])

    first_row = lax.axis_index("strip") * rows + jnp.where(after, rows - EDGE, 0)
    row = lax.broadcasted_iota(jnp.int32, (EDGE, LANES), 0) + first_row
    height = rows * lax.axis_size("strip")
    combine(down, 0, EDGE, coefs, row, height, halo.shape[2], store)


def first_kernel(rows, halo, taps, coefs, out, padded, down):
    def store(side, matched, spread):
        out[side] = matched
        out[2 + side] = spread

    halo_part(halo, strip_is_even(), taps, coefs, padded, down, rows, store)


def weight_kernel(own, first, halo, taps, coefs, out, padded, down, second):
    rows = own.shape[1]
    even = strip_is_even()

    def store(side, matched, spread):
        second[side] = matched
        second[2 + side] = spread

    halo_part(halo, jnp.logical_not(even), taps, coefs, padded, down, rows, store)
    for extra, start in (
        (first, jnp.where(even, rows - EDGE, 0)),
        (None, EDGE),
        (second, jnp.where(even, 0, rows - EDGE)),
    ):
        count = EDGE if extra is not None else rows - 2 * EDGE
        start = pl.multiple_of(start, EDGE) if extra is not None else start
        for side in range(2):
            matched = own[side, pl.ds(start, count), :]
            spread = own[2 + side, pl.ds(start, count), :]
            if extra is not None:
                matched = matched + extra[side]
                spread = spread + extra[2 + side]
            out[pl.ds(4 * start + side, count, stride=4), :] = matched
            out[pl.ds(4 * start + 2 + side, count, stride=4), :] = 1.0 / spread


def owner_kernel(moved, coadd, depth):
    visits = moved.shape[0] // 4
    for side in range(2):
        matched = moved[pl.ds(side, visits, stride=4), :]
        weight = moved[pl.ds(2 + side, visits, stride=4), :]
        valid = weight > 0.0
        visit = lax.broadcasted_iota(jnp.int32, matched.shape, 0)

        def extreme(values, value):
            first = jnp.min(jnp.where(values == value, visit, visits), axis=0, keepdims=True)
            return jnp.sum(jnp.where(visit == first, weight, 0.0), axis=0, keepdims=True)

        low_values = jnp.where(valid, matched, jnp.inf)
        high_values = jnp.where(valid, matched, -jnp.inf)
        low_value = jnp.min(low_values, axis=0, keepdims=True)
        high_value = jnp.max(high_values, axis=0, keepdims=True)
        low_weight = extreme(low_values, low_value)
        high_weight = extreme(high_values, high_value)
        total = jnp.sum(weight * matched, axis=0, keepdims=True)
        weights = jnp.sum(weight, axis=0, keepdims=True)
        lanes = slice(side * LANES, (side + 1) * LANES)
        coadd[:, lanes] = (total - low_weight * low_value - high_weight * high_value) / (
            weights - low_weight - high_weight
        )
        depth[:, lanes] = jnp.log(weights + 1.0)


VMEM = pl.BlockSpec(memory_space=pltpu.VMEM)
HBM = pl.BlockSpec(memory_space=pltpu.HBM)
SMEM = pl.BlockSpec(memory_space=pltpu.SMEM)
PARAMS = pltpu.CompilerParams(vmem_limit_bytes=VMEM_LIMIT)


def f32(*shape):
    return jax.ShapeDtypeStruct(shape, jnp.float32)


def cost(flops):
    return pl.CostEstimate(flops=flops, bytes_accessed=1 << 20, transcendentals=0)


def loaded(images, variances):
    width = images.shape[2]
    return pl.pallas_call(
        load_kernel,
        in_specs=[HBM] * 2,
        out_specs=[VMEM] * 4,
        out_shape=[f32(*images.shape)] * 2 + [f32(2, EDGE, width)] * 2,
        scratch_shapes=[pltpu.SemaphoreType.DMA((2,))],
        compiler_params=PARAMS,
    )(*(pltpu.with_memory_space_constraint(x, pltpu.HBM) for x in (images, variances)))


def strip_parts(ids, kernels, amplitudes, shapes, images, variances, masks):
    rows = images.shape[1]
    return pl.pallas_call(
        strip_kernel,
        in_specs=[SMEM, VMEM] + [HBM] * 2 + [VMEM] * 2 + [HBM],
        out_specs=[VMEM] * 3,
        out_shape=[f32(4, rows, LANES), f32(9, *kernels.shape[1:3], LANES), f32(18, LANES)],
        scratch_shapes=[
            pltpu.VMEM((3, 2, rows + 2 * EDGE, LANES), jnp.float32),
            pltpu.VMEM((9, 2, rows, LANES), jnp.float32),
            pltpu.VMEM(amplitudes.shape, jnp.float32),
            pltpu.VMEM(shapes.shape, jnp.float32),
            pltpu.VMEM(masks.shape, jnp.int32),
            pltpu.SemaphoreType.DMA((3,)),
        ],
        compiler_params=PARAMS,
        cost_estimate=cost(20_000_000),
    )(
        ids,
        kernels,
        pltpu.with_memory_space_constraint(amplitudes, pltpu.HBM),
        pltpu.with_memory_space_constraint(shapes, pltpu.HBM),
        images,
        variances,
        pltpu.with_memory_space_constraint(masks, pltpu.HBM),
    )


HALO_SCRATCH = [
    pltpu.VMEM((9, 2, 3 * EDGE, LANES), jnp.float32),
    pltpu.VMEM((9, 2, EDGE, LANES), jnp.float32),
]


def first_part(rows, halo, taps, coefs):
    return pl.pallas_call(
        functools.partial(first_kernel, rows),
        in_specs=[VMEM] * 3,
        out_specs=VMEM,
        out_shape=f32(4, EDGE, LANES),
        scratch_shapes=HALO_SCRATCH,
        compiler_params=PARAMS,
        cost_estimate=cost(4_000_000),
    )(halo, taps, coefs)


def weighted(own, first, halo, taps, coefs):
    rows = own.shape[1]
    return pl.pallas_call(
        weight_kernel,
        in_specs=[VMEM] * 5,
        out_specs=VMEM,
        out_shape=f32(4 * rows, LANES),
        scratch_shapes=HALO_SCRATCH + [pltpu.VMEM((4, EDGE, LANES), jnp.float32)],
        compiler_params=PARAMS,
    )(own, first, halo, taps, coefs)


def owned(moved, width):
    return pl.pallas_call(
        owner_kernel,
        in_specs=[VMEM],
        out_specs=[VMEM, VMEM],
        out_shape=[f32(1, width)] * 2,
        compiler_params=PARAMS,
    )(moved)


def before_exchange(images, variances, masks, visit_ids, kernels, amplitudes, shapes):
    strips = lax.axis_size("strip")
    rows = images.shape[1]
    image_rows, variance_rows, sent_first, sent_second = loaded(images, variances)
    tables = (
        jnp.transpose(kernels, (1, 3, 2, 0)),
        jnp.transpose(amplitudes, (1, 0)),
        jnp.transpose(shapes, (2, 1, 0)),
    )

    def swap(edge, start):
        pairs = [(i, i + 1) for i in range(start, strips - 1, 2)]
        return lax.ppermute(edge, "strip", pairs + [(b, a) for a, b in pairs])

    halo_first = swap(sent_first, 0)
    halo_second = swap(sent_second, 1)
    own, taps, coefs = strip_parts(visit_ids, *tables, image_rows, variance_rows, masks)
    first = first_part(rows, halo_first, taps, coefs)
    return weighted(own, first, halo_second, taps, coefs)


def shards(images, variances, masks, visit_ids, kernels, amplitudes, shapes):
    rows, width = images.shape[1:]
    visits = lax.axis_size("visit")
    sent = before_exchange(images, variances, masks, visit_ids, kernels, amplitudes, shapes)
    moved = lax.all_to_all(
        sent.reshape(rows, 4, LANES), "visit", split_axis=0, concat_axis=0, tiled=True
    )
    coadd, depth = owned(moved.reshape(visits * 4, LANES), width)
    return coadd, depth


def solution(mesh):
    in_specs = (
        P("visit", "strip", None),
        P("visit", "strip", None),
        P("visit", "strip", None),
        P("visit"),
        P(),
        P(),
        P(),
    )
    out_specs = (P(("strip", "visit"), None), P(("strip", "visit"), None))
    return jax.shard_map(shards, mesh=mesh, in_specs=in_specs, out_specs=out_specs, check_vma=False)
```
